128 devices in a mesh: fsdp: 8 (over y_lo, x), rep: 16 (over z, y_hi, core).
Axes of the slice: x: 4, y: 4 (y_hi: 2, y_lo: 2; y = y_hi * 2 + y_lo), z: 4, core: 2. Of those that a mesh axis runs over, the one named last changes fastest.
Arguments:
- partial_grads: bfloat16 [16, 8, 2, 256, 8192], P('rep', 'fsdp'), may hold values from -400 to 400
- params: float32 [2, 256, 8192], P(None, 'fsdp'), may hold values from -4 to 4
- moment: float32 [2, 256, 8192], P(None, 'fsdp'), may hold values from -3 to 3
- second_moment: float32 [2, 256, 8192], P(None, 'fsdp'), may hold values from 0.05 to 1
- snapshot: float32 [16, 2, 256, 8192], P('rep', None, 'fsdp'), may hold values from -6 to 6
Outputs:
- new_params: float32 [2, 256, 8192], P(None, 'fsdp')
- new_moment: float32 [2, 256, 8192], P(None, 'fsdp')
- new_second: float32 [2, 256, 8192], P(None, 'fsdp')
- held_delta: float32 [16, 2, 256, 8192], P('rep', None, 'fsdp')
The draws below stay inside these ranges and needn't reach their ends.
All inputs are finite; a program needn't handle non-finite values.
Results may differ from the reference program's by a relative error of at most 0.0028.
Values may be sent and summed in bfloat16 or wider, within the bound.
No kernel may reach another device: no remote copies, remote signals or barrier semaphores. Data moves between devices by JAX's collectives and lax.ppermute only.
A program may use at most 128 MiB of HBM per device.

```python
import math
import jax
import jax.numpy as jnp
from jax import lax

D = 8192
QBLOCK = 128
LAYERS = 2
FSDP_WAYS = 8
REPLICAS = 16
ROWS = 256


def base_weights(key):
    return jax.random.truncated_normal(key, -4.0, 4.0, (LAYERS, ROWS, D))


def draw_partial_grads(key, part):
    key = jax.random.fold_in(key, 11)
    k_rows, k_cols, k_base = jax.random.split(key, 3)
    position = (jnp.arange(ROWS, dtype=jnp.float32) + 0.5) / ROWS
    jitter = jax.random.uniform(k_rows, (LAYERS, ROWS), minval=-0.05, maxval=0.05)
    col_power = jax.random.uniform(k_cols, (D,))
    base = jax.random.truncated_normal(k_base, -4.0, 4.0, (REPLICAS, FSDP_WAYS, LAYERS, ROWS, D))
    row_scale = 10.0 ** (position[None, :] + jitter)
    mixed = base
    level = 0.3
    scale = level * row_scale[:, :, None] * (10.0 ** col_power)[None, None, :]
    return (mixed * scale[None, None]).astype(jnp.bfloat16)


def draw_params(key, part):
    shared = base_weights(key)
    return shared


def draw_snapshot(key, part):
    shared = base_weights(key)
    key = jax.random.fold_in(key, 31)
    k_age, k_drift = jax.random.split(key)
    age = 10.0 ** jax.random.uniform(k_age, (REPLICAS, 1, 1, 1), minval=-2.3, maxval=-1.3)
    drift = jax.random.truncated_normal(k_drift, -4.0, 4.0, (REPLICAS, LAYERS, ROWS, D))
    return shared[None] - age * drift


def block_scale(key, dims, shards, low, largest):
    loudness, own = 1.0, jax.random.fold_in(key, 6)
    for dim, blocks in shards:
        draws = jnp.exp(jax.random.uniform(jax.random.fold_in(own, dim), (blocks,), jnp.float32, low / len(shards), largest / len(shards)))
        loudness = loudness * jnp.repeat(draws, dims[dim] // blocks).reshape([-1 if axis == dim else 1 for axis in range(len(dims))])
    return loudness


def gaussian(key, extent, deviation, limit, shards=(), kind=jnp.bfloat16):
    array = jax.random.normal(key, extent, jnp.float32) * deviation
    if len(shards) > 0:
        array = block_scale(key, extent, shards, -0.22, 0.18) * array
    return jnp.clip(array, min=-limit, max=limit).astype(kind)


def setup_inputs(seed: int = 0) -> dict:
    key_list = jax.random.split(jax.random.key(seed), 6)
    partial_grads = draw_partial_grads(jax.random.fold_in(key_list[5], 71), 0)
    params = draw_params(jax.random.fold_in(key_list[5], 71), 0)
    moment = gaussian(key_list[2], (LAYERS, ROWS, D), 0.5, 3.0, ((1, 8),), jnp.float32)
    second_moment = jnp.clip(jnp.exp(math.log(1.0) - 2.9957323 * jax.random.uniform(key_list[3], (LAYERS, ROWS, D), jnp.float32) ** block_scale(key_list[3], (LAYERS, ROWS, D), ((1, 8),), -0.2, 0.2)), 0.05, 1.0)
    snapshot = draw_snapshot(jax.random.fold_in(key_list[5], 71), 0)
    return dict(partial_grads=partial_grads, params=params, moment=moment, second_moment=second_moment, snapshot=snapshot)


beta_first = 0.9
beta_second = 0.95
learn_rate = 0.02
decay_rate = 0.1
adam_eps = 1e-08
scale_eps = 1e-06
rms_eps = 1e-06

def reference(partial_grads, params, moment, second_moment, snapshot):

    def accumulate(index, running):
        return running + lax.optimization_barrier(jnp.sum(partial_grads[index].astype(jnp.float32), axis=0))
    reduced = lax.fori_loop(0, REPLICAS, accumulate, jnp.zeros((LAYERS, ROWS, D), jnp.float32))
    squares = jnp.sum(reduced * reduced)
    grad_rms = jnp.sqrt(squares / (LAYERS * ROWS * D) + rms_eps)
    clip_factor = 1.0 / grad_rms
    clipped = clip_factor * reduced
    new_moment = beta_first * moment + (1.0 - beta_first) * clipped
    new_second = beta_second * second_moment + (1.0 - beta_second) * clipped * clipped
    new_params = params - learn_rate * (new_moment / (jnp.sqrt(new_second) + adam_eps) + decay_rate * params)
    weight_delta = new_params[None] - snapshot
    blocks = weight_delta.reshape(REPLICAS, LAYERS, ROWS, D // QBLOCK, QBLOCK)
    scales = (lax.optimization_barrier(jnp.max(jnp.abs(blocks), axis=-1)) + scale_eps).astype(jnp.bfloat16)
    scales = lax.optimization_barrier(scales)
    wide_scales = scales.astype(jnp.float32)[..., None]
    code_words = lax.optimization_barrier((blocks / wide_scales).astype(jnp.bfloat16))
    decoded = (code_words.astype(jnp.float32) * wide_scales).reshape(REPLICAS, LAYERS, ROWS, D)
    held_delta = jnp.roll(decoded, 1, axis=0)
    return (new_params, new_moment, new_second, held_delta)
```

```python
import jax
import jax.numpy as jnp
from jax import lax
from jax.sharding import PartitionSpec as P

QBLOCK = 128
AXES = ("fsdp", "rep")

beta_first = 0.9
beta_second = 0.95
learn_rate = 0.02
decay_rate = 0.1
adam_eps = 1e-08
scale_eps = 1e-06
rms_eps = 1e-06


def spots():
    return [
        (x, yl + 2 * yh, z, c)
        for yl in range(2)
        for x in range(4)
        for z in range(4)
        for yh in range(2)
        for c in range(2)
    ]


def rank(x, y, z, c):
    x, y, z, c = x % 4, y % 4, z % 4, c % 2
    return ((y % 2) * 4 + x) * 16 + z * 4 + (y // 2) * 2 + c


def move(value, x=0, y=0, z=0, c=0):
    pairs = [(rank(*s), rank(s[0] + x, s[1] + y, s[2] + z, s[3] + c)) for s in spots()]
    return lax.ppermute(value, AXES, pairs)


def pick(value, index, axis):
    return lax.dynamic_index_in_dim(value, index, axis, keepdims=False)


def wide(value):
    return value.astype(jnp.float32)


def narrow(value):
    return value.astype(jnp.bfloat16)


def exchange(value, axis, me, name):
    own = pick(value, me, axis)
    got = [
        move(narrow(pick(value, (me + k) % 4, axis)), **{name: k}) for k in (1, 3, 2)
    ]
    for g in got:
        own = own + wide(g)
    return own


def local(partial_grads, params, moment, second_moment, snapshot):
    fsdp = lax.axis_index("fsdp")
    rep = lax.axis_index("rep")
    x, yl = fsdp % 4, fsdp // 4
    z, yh, c = rep // 4, (rep // 2) % 2, rep % 2
    grads = partial_grads[0, 0]
    swapped = move(pick(grads, 1 - c, 0), c=1)
    base = narrow(params - snapshot[0])
    held_base = lax.ppermute(base, "rep", [(i, (i + 1) % 16) for i in range(16)])

    total = wide(pick(grads, c, 0)) + wide(swapped)
    total = total.reshape(2, 4, 4, 8, 8192)
    left, right = total[..., :4096], total[..., 4096:]
    left = exchange(left, 1, x, "x")
    right = exchange(right, 2, z, "z")
    left = exchange(left, 1, z, "z")
    right = exchange(right, 1, x, "x")
    both = jnp.concatenate([left, right], axis=-1)
    other = narrow(pick(both, 1 - yl, 0))
    mine = pick(both, yl, 0)
    mine = narrow(mine)
    side = wide(move(other, y=1)) + wide(move(other, y=3))
    piece = (wide(mine) + wide(move(mine, y=2))) + side

    squares = jnp.sum(piece * piece).reshape(1, 1)
    for name in ("x", "z"):
        side = move(squares, **{name: 1}) + move(squares, **{name: 3})
        squares = (squares + move(squares, **{name: 2})) + side
    squares = squares + move(squares, c=1)
    fs = [(i, (i + 4) % 8) for i in range(8)]
    squares = squares + lax.ppermute(squares, "fsdp", fs)

    small = narrow(piece)
    ring = jnp.stack([small] + [move(small, z=k) for k in (1, 2, 3)])
    ring = jnp.stack([pick(ring, (z - j) % 4, 0) for j in range(4)])
    ring = ring.reshape(32, 8192)
    swap = move(ring, c=1)
    reduced = wide(jnp.stack([jnp.where(c == 0, ring, swap), jnp.where(c == 0, swap, ring)]))

    clip_factor = lax.rsqrt(squares[0, 0] / (2 * 256 * 8192) + rms_eps)
    clipped = clip_factor * reduced
    new_moment = beta_first * moment + (1.0 - beta_first) * clipped
    new_second = beta_second * second_moment + (1.0 - beta_second) * clipped * clipped
    change = -learn_rate * (
        new_moment / (jnp.sqrt(new_second) + adam_eps) + decay_rate * params
    )
    new_params = params + change
    delta = change + wide(held_base)
    blocks = delta.reshape(2, 32, 64, QBLOCK)
    scales = narrow(jnp.max(jnp.abs(blocks), axis=-1) + scale_eps)
    scales = wide(lax.optimization_barrier(scales))[..., None]
    codes = lax.optimization_barrier(narrow(blocks / scales))
    held = (wide(codes) * scales).reshape(1, 2, 32, 8192)
    return (new_params, new_moment, new_second, held)


def solution(mesh):
    return jax.shard_map(
        local,
        mesh=mesh,
        in_specs=(
            P("rep", "fsdp", None, None, None),
            P(None, "fsdp", None),
            P(None, "fsdp", None),
            P(None, "fsdp", None),
            P("rep", None, "fsdp", None),
        ),
        out_specs=(
            P(None, "fsdp", None),
            P(None, "fsdp", None),
            P(None, "fsdp", None),
            P("rep", None, "fsdp", None),
        ),
        check_vma=False,
    )
```

```python
import jax
import jax.numpy as jnp
from jax import lax
from jax.experimental import pallas as pl
from jax.experimental.pallas import tpu as pltpu
from jax.sharding import Mesh, PartitionSpec as P

QBLOCK = 128
AXES = ("yl", "x", "z", "yh", "c")
FSDP = ("yl", "x")
REP = ("z", "yh", "c")
MIB = 1 << 20

beta_first = 0.9
beta_second = 0.95
learn_rate = 0.02
decay_rate = 0.1
adam_eps = 1e-08
scale_eps = 1e-06
rms_eps = 1e-06

BF16 = jnp.bfloat16
F32 = jnp.float32


def spots():
    return [
        (x, yl + 2 * yh, z, c)
        for yl in range(2)
        for x in range(4)
        for z in range(4)
        for yh in range(2)
        for c in range(2)
    ]


def rank(x, y, z, c):
    x, y, z, c = x % 4, y % 4, z % 4, c % 2
    return ((y % 2) * 4 + x) * 16 + z * 4 + (y // 2) * 2 + c


def move(value, x=0, y=0, z=0, c=0):
    pairs = [(rank(*s), rank(s[0] + x, s[1] + y, s[2] + z, s[3] + c)) for s in spots()]
    return lax.ppermute(value, AXES, pairs)


def swap_x(value, mask):
    pairs = [(rank(*s), rank(s[0] ^ mask, *s[1:])) for s in spots()]
    return lax.ppermute(value, AXES, pairs)


def move_yl(value, c=0):
    pairs = [(rank(*s), rank(s[0], s[1] ^ 1, s[2], s[3] + c)) for s in spots()]
    return lax.ppermute(value, AXES, pairs)


def wide(value):
    return value.astype(F32)


def narrow(value):
    return value.astype(BF16)


def vmem_call(body, where, arrays, outs, after=()):
    count = len(arrays)

    def run(where, *refs):
        body(where, *refs[:count], *refs[count + len(after) :])

    arrays = [pltpu.with_memory_space_constraint(a, pltpu.VMEM) for a in arrays]
    return pl.pallas_call(
        run,
        in_specs=[pl.BlockSpec(memory_space=pltpu.SMEM)]
        + [pl.BlockSpec(memory_space=pltpu.VMEM)] * count
        + [pl.BlockSpec(memory_space=pl.ANY)] * len(after),
        out_specs=[pl.BlockSpec(memory_space=pltpu.VMEM)] * len(outs),
        out_shape=[pltpu.VMEM(dims, kind) for dims, kind in outs],
        compiler_params=pltpu.CompilerParams(vmem_limit_bytes=12 * MIB),
        cost_estimate=pl.CostEstimate(flops=4 * MIB, bytes_accessed=4 * MIB, transcendentals=0),
    )(where, *arrays, *after)


LEFT = (2, 16, 10240)
RIGHT = (8, 16, 1536)
ORDER = (0, 2, 1, 3)

X, YL, Z, C = range(4)


def fetch(grads, where, wanted, after=()):
    def body(where, src, *refs):
        outs, sems = refs[len(after) : -1], refs[-1]
        copies = []
        for out, (own, left, offsets) in zip(outs, wanted):
            layer = where[C] if own else 1 - where[C]
            for i, k in enumerate(offsets):
                if left:
                    row = (where[X] + k) % 4
                    for f in range(2):
                        src_row, dst_row = src.at[layer, f, row], out.at[i, f]
                        copies.append((src_row.at[pl.ds(0, 16)], dst_row.at[:, pl.ds(0, 8192)]))
                        for part in range(4):
                            thin = pl.ds(2048 * part + 1536, 512)
                            to = pl.ds(8192 + 512 * part, 512)
                            copies.append((src_row.at[pl.ds(16, 16), thin], dst_row.at[:, to]))
                else:
                    cols = pl.ds(pl.multiple_of((where[Z] + k) % 4 * 2048, 2048), 1536)
                    for f in range(8):
                        copies.append(
                            (src.at[layer, f // 4, f % 4, pl.ds(16, 16), cols], out.at[i, f])
                        )
        copies = [pltpu.make_async_copy(a, b, sems.at[i]) for i, (a, b) in enumerate(copies)]
        for copy in copies:
            copy.start()
        for copy in copies:
            copy.wait()

    blocks = sum(len(offsets) for _, _, offsets in wanted)
    grads = pltpu.with_memory_space_constraint(grads.reshape(2, 2, 4, 32, 8192), pltpu.HBM)
    return pl.pallas_call(
        body,
        in_specs=[pl.BlockSpec(memory_space=pltpu.SMEM)]
        + [pl.BlockSpec(memory_space=pl.ANY)] * (1 + len(after)),
        out_specs=[pl.BlockSpec(memory_space=pl.ANY)] * len(wanted),
        out_shape=[
            pltpu.VMEM((len(offsets),) + (LEFT if left else RIGHT), BF16)
            for _, left, offsets in wanted
        ],
        scratch_shapes=[pltpu.SemaphoreType.DMA((16 * blocks,))],
        compiler_params=pltpu.CompilerParams(vmem_limit_bytes=4 * MIB),
        cost_estimate=pl.CostEstimate(flops=0, bytes_accessed=blocks * MIB, transcendentals=0),
    )(where, grads, *after)


def preload(arrays, where, before):
    count = len(arrays)

    def body(where, *refs):
        ins, outs, sems = refs[:count], refs[count + 1 : -1], refs[-1]
        copies = [
            pltpu.make_async_copy(
                a.at[l, pl.ds(8 * r, 8)], b.at[l, pl.ds(8 * r, 8)], sems.at[i, l, r]
            )
            for i, (a, b) in enumerate(zip(ins, outs))
            for l in range(2)
            for r in range(4)
        ]
        for copy in copies:
            copy.start()
        for copy in copies:
            copy.wait()

    arrays = [pltpu.with_memory_space_constraint(a, pltpu.HBM) for a in arrays]
    return pl.pallas_call(
        body,
        in_specs=[pl.BlockSpec(memory_space=pltpu.SMEM)]
        + [pl.BlockSpec(memory_space=pl.ANY)] * (count + 1),
        out_specs=[pl.BlockSpec(memory_space=pl.ANY)] * count,
        out_shape=[pltpu.VMEM(a.shape, a.dtype) for a in arrays],
        scratch_shapes=[pltpu.SemaphoreType.DMA((count, 2, 4))],
        compiler_params=pltpu.CompilerParams(vmem_limit_bytes=4 * MIB),
        cost_estimate=pl.CostEstimate(flops=MIB, bytes_accessed=6 * MIB, transcendentals=0),
    )(where, *arrays, before)


def add(*terms):
    total = terms[0]
    for t in terms[1:]:
        total = total + t
    return total


def total_of(refs, *index):
    return add(*[wide(r[index] if index else r[...]) for r in refs])


def pair_sum(where, mine, theirs, after=()):
    dims = mine.shape[1:]

    def body(where, a, b, *outs):
        for i, out in enumerate(outs):
            out[...] = narrow(wide(a[i]) + wide(b[i]))

    return list(vmem_call(body, where, (mine, theirs), [(dims, BF16)] * 3, after))


def split(where, arrays, whole, cut, width, after=()):
    dims = (2, 16, width)
    count = len(arrays)

    def body(where, *refs):
        ins = list(refs[:count]) + [r.at[3] for r in refs[count:-4]]
        for out, k in zip(refs[-4:], ORDER):
            for first, last, index in cut(where, k):
                out[:, :, first:last] = total_of(ins, *index).astype(out.dtype)

    outs = [(dims, F32)] + [(dims, BF16)] * 3
    return list(vmem_call(body, where, list(arrays) + whole, outs, after))


def travel(blocks, name):
    return [move(b, **{name: k}) for k, b in zip(ORDER[1:], blocks)]


def update(where, layer, j, pieces, state, outs):
    sq, p, m, v, base = state
    clip_factor = lax.rsqrt(sq[0:1, 0:1] / (2 * 256 * 8192) + rms_eps)
    place = (where[Z] - j + 4) % 4
    for g in range(2048 // QBLOCK):
        cols = pl.ds(pl.multiple_of(j * 2048 + g * QBLOCK, QBLOCK), QBLOCK)
        clipped = clip_factor * wide(pieces[place, :, g * QBLOCK : (g + 1) * QBLOCK])
        new_m = beta_first * m[layer, :, cols] + (1.0 - beta_first) * clipped
        new_v = beta_second * v[layer, :, cols] + (1.0 - beta_second) * clipped * clipped
        old = p[layer, :, cols]
        change = -learn_rate * (new_m / (jnp.sqrt(new_v) + adam_eps) + decay_rate * old)
        outs[0][:, cols] = old + change
        outs[1][:, cols] = new_m
        outs[2][:, cols] = new_v
        delta = change + wide(base[layer, :, cols])
        scale = jnp.max(jnp.abs(delta), axis=1, keepdims=True) + scale_eps
        scale = wide(narrow(scale))
        outs[3][:, cols] = wide(narrow(delta / scale)) * scale


def update_all(where, ours, theirs, state):
    def body(where, ours, theirs, *refs):
        state, outs, held, sems = refs[:5], refs[5:9], refs[9:13], refs[13]

        def copies(side, j):
            layer = where[C] if side == 0 else 1 - where[C]
            cols = pl.ds(pl.multiple_of(j * 2048, 2048), 2048)
            return [
                pltpu.make_async_copy(
                    held[i].at[side, :, cols], outs[i].at[layer, :, cols], sems.at[i, side, j]
                )
                for i in range(4)
            ]

        for side, pieces in enumerate((ours, theirs)):

            @pl.loop(0, 4)
            def _(j, side=side, pieces=pieces):
                layer = where[C] if side == 0 else 1 - where[C]
                update(where, layer, j, pieces, state, [h.at[side] for h in held])
                for copy in copies(side, j):
                    copy.start()

        for side in range(2):
            for j in range(4):
                for copy in copies(side, j):
                    copy.wait()

    arrays = [pltpu.with_memory_space_constraint(a, pltpu.VMEM) for a in [ours, theirs, *state]]
    return pl.pallas_call(
        body,
        in_specs=[pl.BlockSpec(memory_space=pltpu.SMEM)]
        + [pl.BlockSpec(memory_space=pltpu.VMEM)] * len(arrays),
        out_specs=[pl.BlockSpec(memory_space=pl.ANY)] * 4,
        out_shape=[pltpu.HBM((2, 32, 8192), F32)] * 4,
        scratch_shapes=[pltpu.VMEM((2, 32, 8192), F32)] * 4 + [pltpu.SemaphoreType.DMA((4, 2, 4))],
        compiler_params=pltpu.CompilerParams(vmem_limit_bytes=14 * MIB),
        cost_estimate=pl.CostEstimate(flops=9 * MIB, bytes_accessed=9 * MIB, transcendentals=0),
    )(where, *arrays)


def local(partial_grads, params, moment, second_moment, snapshot):
    where = jnp.stack([lax.axis_index(name) for name in ("x", "yl", "z", "c")]).astype(jnp.int32)
    grads = partial_grads[0, 0]

    order = ORDER[1:] + (0,)
    theirs = fetch(grads, where, [(False, True, order)])
    theirs += fetch(grads, where, [(False, False, order)], theirs)
    theirs = [move(b, c=1) for b in theirs]
    base = narrow(params - snapshot[0])
    held_base = lax.ppermute(base, REP, [(i, (i + 1) % 16) for i in range(16)])
    mine = fetch(grads, where, [(True, True, order)], (base,))
    left = pair_sum(where, mine[0], theirs[0])
    mine += fetch(grads, where, [(True, False, order)], (left[0],))
    right = pair_sum(where, mine[1], theirs[1], (held_base,))
    state = preload([params, moment, second_moment], where, right[0])
    left = travel(left, "x")
    right = travel(right, "z")

    def by_z(where, k):
        block = (where[Z] + k) % 4
        wide_part = pl.ds(pl.multiple_of(block * 2048, 2048), 2048)
        thin_part = pl.ds(pl.multiple_of(8192 + block * 512, 512), 512)
        every = slice(None)
        return (0, 2048, (every, every, wide_part)), (2048, 2560, (every, every, thin_part))

    def by_x(where, k):
        return ((0, 1536, (slice(None), (where[X] + k) % 4)),)

    left = split(where, left, [mine[0], theirs[0]], by_z, 2560, (state[0],))
    ready = left[1]
    left = left[:1] + travel(left[1:], "z")
    whole = [a.reshape(4, 2, 4, 16, 1536) for a in (mine[1], theirs[1])]
    right = split(where, [r.reshape(2, 4, 16, 1536) for r in right], whole, by_x, 1536, (ready,))
    right = right[:1] + travel(right[1:], "x")

    def join(where, *refs):
        for out, index in ((refs[8], where[YL]), (refs[9], 1 - where[YL])):
            a = narrow(total_of(refs[:4], index))
            out[:16, :] = a[:, :2048]
            out[16:, :1536] = narrow(total_of(refs[4:8], index))
            out[16:, 1536:] = a[:, 2048:]

    mine, other = vmem_call(join, where, left + right, [((32, 2048), BF16)] * 2)
    fourth = [mine, move(mine, y=2), move(other, y=1), move(other, y=3)]

    def finish(where, a, b, d, e, out):
        total = (wide(a[...]) + wide(b[...])) + (wide(d[...]) + wide(e[...]))
        squares = jnp.sum(jnp.sum(total * total, axis=0, keepdims=True), axis=1, keepdims=True)
        out[:, :2048] = narrow(total)
        high = wide(narrow(squares))
        middle = wide(narrow(squares - high))
        low = squares - high - middle
        lane = lax.broadcasted_iota(jnp.int32, (32, 128), 1)
        tail = jnp.where(lane == 0, high, jnp.where(lane == 1, middle, jnp.where(lane == 2, low, 0.0)))
        out[:, 2048:] = narrow(tail)

    piece = vmem_call(finish, where, fourth, [((32, 2176), BF16)])[0]
    ring = [piece] + [move(piece, z=k) for k in (2, 1, 3)]

    def gather(where, *refs):
        ins, out, squares = refs[:4], refs[4], refs[5]
        parts = [jnp.sum(wide(ref[:16, 2048:])[:8, :], axis=1, keepdims=True) for ref in ins]
        for k, ref in zip(ORDER, ins):
            out[k] = ref[:, :2048]
        total = (parts[0] + parts[1]) + (parts[2] + parts[3])
        squares[...] = jnp.broadcast_to(total, (8, 128))

    ours, squares = vmem_call(gather, where, ring, [((4, 32, 2048), BF16), ((8, 128), F32)])
    theirs = move(ours, c=1)
    squares = squares + swap_x(squares, 1)
    squares = squares + swap_x(squares, 3)
    side = move_yl(squares) + move_yl(squares, c=1)
    squares = (squares + move(squares, c=1)) + side
    outs = update_all(where, ours, theirs, [squares, *state, held_base])
    return (outs[0], outs[1], outs[2], outs[3][None])


def solution(mesh):
    fine = Mesh(mesh.devices.reshape(2, 4, 4, 2, 2), AXES)
    row = P(None, FSDP, None)
    held = P(REP, None, FSDP, None)
    return jax.shard_map(
        local,
        mesh=fine,
        in_specs=(P(REP, FSDP, None, None, None), row, row, row, held),
        out_specs=(row, row, row, held),
        check_vma=False,
    )
```

```python
import jax
import jax.numpy as jnp
from jax import lax
from jax.experimental import pallas as pl
from jax.experimental.pallas import tpu as pltpu
from jax.sharding import Mesh, PartitionSpec as P

QBLOCK = 128
AXES = ("yl", "x", "z", "yh", "c")
FSDP = ("yl", "x")
REP = ("z", "yh", "c")
MIB = 1 << 20

beta_first = 0.9
beta_second = 0.95
learn_rate = 0.02
decay_rate = 0.1
adam_eps = 1e-08
scale_eps = 1e-06
rms_eps = 1e-06

BF16 = jnp.bfloat16
F32 = jnp.float32


def spots():
    return [
        (x, yl + 2 * yh, z, c)
        for yl in range(2)
        for x in range(4)
        for z in range(4)
        for yh in range(2)
        for c in range(2)
    ]


def rank(x, y, z, c):
    x, y, z, c = x % 4, y % 4, z % 4, c % 2
    return ((y % 2) * 4 + x) * 16 + z * 4 + (y // 2) * 2 + c


def move(value, x=0, y=0, z=0, c=0):
    pairs = [(rank(*s), rank(s[0] + x, s[1] + y, s[2] + z, s[3] + c)) for s in spots()]
    return lax.ppermute(value, AXES, pairs)


def swap_x(value, mask):
    pairs = [(rank(*s), rank(s[0] ^ mask, *s[1:])) for s in spots()]
    return lax.ppermute(value, AXES, pairs)


def move_yl(value, c=0):
    pairs = [(rank(*s), rank(s[0], s[1] ^ 1, s[2], s[3] + c)) for s in spots()]
    return lax.ppermute(value, AXES, pairs)


def wide(value):
    return value.astype(F32)


def narrow(value):
    return value.astype(BF16)


def vmem_call(body, where, arrays, outs, after=()):
    count = len(arrays)

    def run(where, *refs):
        body(where, *refs[:count], *refs[count + len(after) :])

    arrays = [pltpu.with_memory_space_constraint(a, pltpu.VMEM) for a in arrays]
    return pl.pallas_call(
        run,
        in_specs=[pl.BlockSpec(memory_space=pltpu.SMEM)]
        + [pl.BlockSpec(memory_space=pltpu.VMEM)] * count
        + [pl.BlockSpec(memory_space=pl.ANY)] * len(after),
        out_specs=[pl.BlockSpec(memory_space=pltpu.VMEM)] * len(outs),
        out_shape=[pltpu.VMEM(dims, kind) for dims, kind in outs],
        compiler_params=pltpu.CompilerParams(vmem_limit_bytes=12 * MIB),
        cost_estimate=pl.CostEstimate(flops=4 * MIB, bytes_accessed=4 * MIB, transcendentals=0),
    )(where, *arrays, *after)


LEFT = (2, 16, 8192)
RIGHT = (8, 16, 2048)
ORDER = (0, 1, 2, 3)
BLOCKS = (0, 1, 2, 3)

X, YL, Z, C = range(4)


def fetch(grads, where, wanted, after=()):
    def body(where, src, *refs):
        outs, sems = refs[len(after) : -1], refs[-1]
        copies = []
        for out, (own, left, offsets) in zip(outs, wanted):
            layer = where[C] if own else 1 - where[C]
            for i, k in enumerate(offsets):
                if left:
                    row = (where[X] + k) % 4
                    for f in range(2):
                        copies.append((src.at[layer, f, row, pl.ds(0, 16)], out.at[i, f]))
                else:
                    cols = pl.ds(pl.multiple_of((where[Z] + k) % 4 * 2048, 2048), 2048)
                    for f in range(8):
                        copies.append(
                            (src.at[layer, f // 4, f % 4, pl.ds(16, 16), cols], out.at[i, f])
                        )
        copies = [pltpu.make_async_copy(a, b, sems.at[i]) for i, (a, b) in enumerate(copies)]
        for copy in copies:
            copy.start()
        for copy in copies:
            copy.wait()

    blocks = sum(len(offsets) for _, _, offsets in wanted)
    grads = pltpu.with_memory_space_constraint(grads.reshape(2, 2, 4, 32, 8192), pltpu.HBM)
    return pl.pallas_call(
        body,
        in_specs=[pl.BlockSpec(memory_space=pltpu.SMEM)]
        + [pl.BlockSpec(memory_space=pl.ANY)] * (1 + len(after)),
        out_specs=[pl.BlockSpec(memory_space=pl.ANY)] * len(wanted),
        out_shape=[
            pltpu.VMEM((len(offsets),) + (LEFT if left else RIGHT), BF16)
            for _, left, offsets in wanted
        ],
        scratch_shapes=[pltpu.SemaphoreType.DMA((8 * blocks,))],
        compiler_params=pltpu.CompilerParams(vmem_limit_bytes=4 * MIB),
        cost_estimate=pl.CostEstimate(flops=0, bytes_accessed=blocks * MIB, transcendentals=0),
    )(where, grads, *after)


def preload(arrays, where, before):
    count = len(arrays)

    def body(where, *refs):
        ins, outs, sems = refs[:count], refs[count + 1 : -1], refs[-1]
        copies = [
            pltpu.make_async_copy(
                a.at[l, pl.ds(8 * r, 8)], b.at[l, pl.ds(8 * r, 8)], sems.at[i, l, r]
            )
            for i, (a, b) in enumerate(zip(ins, outs))
            for l in range(2)
            for r in range(4)
        ]
        for copy in copies:
            copy.start()
        for copy in copies:
            copy.wait()

    arrays = [pltpu.with_memory_space_constraint(a, pltpu.HBM) for a in arrays]
    return pl.pallas_call(
        body,
        in_specs=[pl.BlockSpec(memory_space=pltpu.SMEM)]
        + [pl.BlockSpec(memory_space=pl.ANY)] * (count + 1),
        out_specs=[pl.BlockSpec(memory_space=pl.ANY)] * count,
        out_shape=[pltpu.VMEM(a.shape, a.dtype) for a in arrays],
        scratch_shapes=[pltpu.SemaphoreType.DMA((count, 2, 4))],
        compiler_params=pltpu.CompilerParams(vmem_limit_bytes=4 * MIB),
        cost_estimate=pl.CostEstimate(flops=MIB, bytes_accessed=6 * MIB, transcendentals=0),
    )(where, *arrays, before)


def add(*terms):
    total = terms[0]
    for t in terms[1:]:
        total = total + t
    return total


def total_of(refs, *index):
    return add(*[wide(r[index] if index else r[...]) for r in refs])


def pair_sum(where, mine, theirs, places, after=()):
    dims = mine.shape[1:]

    def body(where, a, b, *outs):
        for out, k in zip(outs, places):
            out[...] = narrow(wide(a[k]) + wide(b[k]))

    return list(vmem_call(body, where, (mine, theirs), [(dims, BF16)] * len(places), after))


def split(where, arrays, whole, cut, after):
    dims = (2, 16, 2048)
    count = len(arrays)

    def body(where, *refs):
        ins = list(refs[:count]) + [r.at[0] for r in refs[count:-4]]
        for out, k in zip(refs[-4:], ORDER):
            out[...] = total_of(ins, *cut(where, k)).astype(out.dtype)

    outs = [(dims, F32)] + [(dims, BF16)] * 3
    return list(vmem_call(body, where, list(arrays) + whole, outs, after))


def travel(blocks, name):
    return [move(b, **{name: k}) for k, b in zip(ORDER[1:], blocks)]


def update(where, layer, j, pieces, state, outs):
    sq, p, m, v, base = state
    clip_factor = lax.rsqrt(sq[0:1, 0:1] / (2 * 256 * 8192) + rms_eps)
    place = (where[Z] - j + 4) % 4
    for g in range(2048 // QBLOCK):
        cols = pl.ds(pl.multiple_of(j * 2048 + g * QBLOCK, QBLOCK), QBLOCK)
        clipped = clip_factor * wide(pieces[place, :, g * QBLOCK : (g + 1) * QBLOCK])
        new_m = beta_first * m[layer, :, cols] + (1.0 - beta_first) * clipped
        new_v = beta_second * v[layer, :, cols] + (1.0 - beta_second) * clipped * clipped
        old = p[layer, :, cols]
        change = -learn_rate * (new_m / (jnp.sqrt(new_v) + adam_eps) + decay_rate * old)
        outs[0][:, cols] = old + change
        outs[1][:, cols] = new_m
        outs[2][:, cols] = new_v
        delta = change + wide(base[layer, :, cols])
        scale = jnp.max(jnp.abs(delta), axis=1, keepdims=True) + scale_eps
        scale = wide(narrow(scale))
        outs[3][:, cols] = wide(narrow(delta / scale)) * scale


def update_all(where, ours, theirs, state):
    def body(where, ours, theirs, *refs):
        state, outs, held, sems = refs[:5], refs[5:9], refs[9:13], refs[13]

        def copies(side, j):
            layer = where[C] if side == 0 else 1 - where[C]
            cols = pl.ds(pl.multiple_of(j * 2048, 2048), 2048)
            return [
                pltpu.make_async_copy(
                    held[i].at[side, :, cols], outs[i].at[layer, :, cols], sems.at[i, side, j]
                )
                for i in range(4)
            ]

        for side, pieces in enumerate((ours, theirs)):

            @pl.loop(0, 4)
            def _(j, side=side, pieces=pieces):
                layer = where[C] if side == 0 else 1 - where[C]
                update(where, layer, j, pieces, state, [h.at[side] for h in held])
                for copy in copies(side, j):
                    copy.start()

        for side in range(2):
            for j in range(4):
                for copy in copies(side, j):
                    copy.wait()

    arrays = [pltpu.with_memory_space_constraint(a, pltpu.VMEM) for a in [ours, theirs, *state]]
    return pl.pallas_call(
        body,
        in_specs=[pl.BlockSpec(memory_space=pltpu.SMEM)]
        + [pl.BlockSpec(memory_space=pltpu.VMEM)] * len(arrays),
        out_specs=[pl.BlockSpec(memory_space=pl.ANY)] * 4,
        out_shape=[pltpu.HBM((2, 32, 8192), F32)] * 4,
        scratch_shapes=[pltpu.VMEM((2, 32, 8192), F32)] * 4 + [pltpu.SemaphoreType.DMA((4, 2, 4))],
        compiler_params=pltpu.CompilerParams(vmem_limit_bytes=14 * MIB),
        cost_estimate=pl.CostEstimate(flops=9 * MIB, bytes_accessed=9 * MIB, transcendentals=0),
    )(where, *arrays)


def local(partial_grads, params, moment, second_moment, snapshot):
    where = jnp.stack([lax.axis_index(name) for name in ("x", "yl", "z", "c")]).astype(jnp.int32)
    grads = partial_grads[0, 0]

    their_right = fetch(grads, where, [(False, False, BLOCKS)])[0]
    got_right = move(their_right, c=1)
    base = narrow(params - snapshot[0])
    held_base = lax.ppermute(base, REP, [(i, (i + 1) % 16) for i in range(16)])
    more = [(own, left, BLOCKS) for own, left in ((True, False), (False, True), (True, True))]
    own_right, their_left, own_left = fetch(grads, where, more, (their_right,))
    got_left = move(their_left, c=1)
    far, near = pair_sum(where, own_right, got_right, (2, 1))
    left = pair_sum(where, own_left, got_left, ORDER[1:], (far,))
    state = preload([params, moment, second_moment], where, left[0])
    left = travel(left, "x")

    def relay(where, far, a, b, out):
        out[...] = narrow(wide(far[...]) + wide(a[3]) + wide(b[3]))

    relayed = [move(far, z=3), own_right, got_right]
    relayed = vmem_call(relay, where, relayed, [(RIGHT, BF16)], (state[0],))[0]
    right = [move(near, z=1), move(relayed, z=3)]

    def by_z(where, k):
        cols = pl.ds(pl.multiple_of((where[Z] + k) % 4 * 2048, 2048), 2048)
        return slice(None), slice(None), cols

    def by_x(where, k):
        return slice(None), (where[X] + k) % 4

    left = split(where, left, [own_left, got_left], by_z, (held_base,))
    ready = left[1]
    left = left[:1] + travel(left[1:], "z")
    whole = [a.reshape(4, 2, 4, 16, 2048) for a in (own_right, got_right)]
    right = split(where, [r.reshape(2, 4, 16, 2048) for r in right], whole, by_x, (ready,))
    right = right[:1] + travel(right[1:], "x")

    def join(where, *refs):
        for out, index in ((refs[8], where[YL]), (refs[9], 1 - where[YL])):
            out[:16, :] = narrow(total_of(refs[:4], index))
            out[16:, :] = narrow(total_of(refs[4:8], index))

    mine, other = vmem_call(join, where, left + right, [((32, 2048), BF16)] * 2)
    fourth = [mine, move(mine, y=2), move(other, y=1), move(other, y=3)]

    def finish(where, a, b, d, e, out):
        total = (wide(a[...]) + wide(b[...])) + (wide(d[...]) + wide(e[...]))
        squares = jnp.sum(jnp.sum(total * total, axis=0, keepdims=True), axis=1, keepdims=True)
        out[:, :2048] = narrow(total)
        high = wide(narrow(squares))
        middle = wide(narrow(squares - high))
        low = squares - high - middle
        lane = lax.broadcasted_iota(jnp.int32, (32, 128), 1)
        tail = jnp.where(lane == 0, high, jnp.where(lane == 1, middle, jnp.where(lane == 2, low, 0.0)))
        out[:, 2048:] = narrow(tail)

    piece = vmem_call(finish, where, fourth, [((32, 2176), BF16)])[0]
    ring = [piece] + [move(piece, z=k) for k in (2, 1, 3)]

    def gather(where, *refs):
        ins, out, squares = refs[:4], refs[4], refs[5]
        parts = [jnp.sum(wide(ref[:16, 2048:])[:8, :], axis=1, keepdims=True) for ref in ins]
        for k, ref in zip((0, 2, 1, 3), ins):
            out[k] = ref[:, :2048]
        total = (parts[0] + parts[1]) + (parts[2] + parts[3])
        squares[...] = jnp.broadcast_to(total, (8, 128))

    ours, squares = vmem_call(gather, where, ring, [((4, 32, 2048), BF16), ((8, 128), F32)])
    theirs = move(ours, c=1)
    side = move(squares, x=1) + move(squares, x=3)
    squares = (squares + move(squares, x=2)) + side
    side = move_yl(squares) + move_yl(squares, c=1)
    squares = (squares + move(squares, c=1)) + side
    outs = update_all(where, ours, theirs, [squares, *state, held_base])
    return (outs[0], outs[1], outs[2], outs[3][None])


def solution(mesh):
    fine = Mesh(mesh.devices.reshape(2, 4, 4, 2, 2), AXES)
    row = P(None, FSDP, None)
    held = P(REP, None, FSDP, None)
    return jax.shard_map(
        local,
        mesh=fine,
        in_specs=(P(REP, FSDP, None, None, None), row, row, row, held),
        out_specs=(row, row, row, held),
        check_vma=False,
    )
```

```python
import jax
import jax.numpy as jnp
from jax import lax
from jax.experimental import pallas as pl
from jax.experimental.pallas import tpu as pltpu
from jax.sharding import Mesh, PartitionSpec as P

QBLOCK = 128
AXES = ("yl", "x", "z", "yh", "c")
FSDP = ("yl", "x")
REP = ("z", "yh", "c")
MIB = 1 << 20

beta_first = 0.9
beta_second = 0.95
learn_rate = 0.02
decay_rate = 0.1
adam_eps = 1e-08
scale_eps = 1e-06
rms_eps = 1e-06

BF16 = jnp.bfloat16
F32 = jnp.float32


def spots():
    return [
        (x, yl + 2 * yh, z, c)
        for yl in range(2)
        for x in range(4)
        for z in range(4)
        for yh in range(2)
        for c in range(2)
    ]


def rank(x, y, z, c):
    x, y, z, c = x % 4, y % 4, z % 4, c % 2
    return ((y % 2) * 4 + x) * 16 + z * 4 + (y // 2) * 2 + c


def move(value, x=0, y=0, z=0, c=0):
    pairs = [(rank(*s), rank(s[0] + x, s[1] + y, s[2] + z, s[3] + c)) for s in spots()]
    return lax.ppermute(value, AXES, pairs)


def turn(value, stage, by, by_z=None):
    by_z = by if by_z is None else by_z

    def goal(x, y, z, c):
        return rank(x + by, y, z, c) if c == stage else rank(x, y, z + by_z, c)

    return lax.ppermute(value, AXES, [(rank(*s), goal(*s)) for s in spots()])


def move_yl(value, c=0):
    pairs = [(rank(*s), rank(s[0], s[1] ^ 1, s[2], s[3] + c)) for s in spots()]
    return lax.ppermute(value, AXES, pairs)


def wide(value):
    return value.astype(F32)


def narrow(value):
    return value.astype(BF16)


def vmem_call(body, where, arrays, outs, after=()):
    count = len(arrays)

    def run(where, *refs):
        body(where, *refs[:count], *refs[count + len(after) :])

    arrays = [pltpu.with_memory_space_constraint(a, pltpu.VMEM) for a in arrays]
    return pl.pallas_call(
        run,
        in_specs=[pl.BlockSpec(memory_space=pltpu.SMEM)]
        + [pl.BlockSpec(memory_space=pltpu.VMEM)] * count
        + [pl.BlockSpec(memory_space=pl.ANY)] * len(after),
        out_specs=[pl.BlockSpec(memory_space=pltpu.VMEM)] * len(outs),
        out_shape=[pltpu.VMEM(dims, kind) for dims, kind in outs],
        compiler_params=pltpu.CompilerParams(vmem_limit_bytes=12 * MIB),
        cost_estimate=pl.CostEstimate(flops=4 * MIB, bytes_accessed=4 * MIB, transcendentals=0),
    )(where, *arrays, *after)


BLOCK = (2, 4, 32, 2048)
ORDER = (0, 1, 2, 3)

X, YL, Z, C = range(4)


def fetch(grads, where, wanted, after=()):
    def body(where, src, *refs):
        outs, sems = refs[len(after) : -1], refs[-1]
        copies = []
        for out, (own, offsets) in zip(outs, wanted):
            layer = where[C] if own else 1 - where[C]
            over_x = layer == 0
            for i, k in enumerate(offsets):
                for yl in range(2):
                    for j in range(4):
                        row = jnp.where(over_x, (where[X] + k) % 4, j)
                        col = jnp.where(over_x, j, (where[Z] + k) % 4)
                        cols = pl.ds(pl.multiple_of(col * 2048, 2048), 2048)
                        copies.append((src.at[layer, yl, row, :, cols], out.at[i, yl, j]))
        copies = [pltpu.make_async_copy(a, b, sems.at[i]) for i, (a, b) in enumerate(copies)]
        for copy in copies:
            copy.start()
        for copy in copies:
            copy.wait()

    blocks = sum(len(offsets) for _, offsets in wanted)
    grads = pltpu.with_memory_space_constraint(grads.reshape(2, 2, 4, 32, 8192), pltpu.HBM)
    return pl.pallas_call(
        body,
        in_specs=[pl.BlockSpec(memory_space=pltpu.SMEM)]
        + [pl.BlockSpec(memory_space=pl.ANY)] * (1 + len(after)),
        out_specs=[pl.BlockSpec(memory_space=pl.ANY)] * len(wanted),
        out_shape=[pltpu.VMEM((len(offsets),) + BLOCK, BF16) for _, offsets in wanted],
        scratch_shapes=[pltpu.SemaphoreType.DMA((8 * blocks,))],
        compiler_params=pltpu.CompilerParams(vmem_limit_bytes=4 * MIB),
        cost_estimate=pl.CostEstimate(flops=0, bytes_accessed=blocks * MIB, transcendentals=0),
    )(where, grads, *after)


def preload(arrays, where, before):
    count = len(arrays)

    def body(where, *refs):
        ins, outs, sems = refs[:count], refs[count + 1 : -1], refs[-1]
        copies = [
            pltpu.make_async_copy(
                a.at[l, pl.ds(8 * r, 8)], b.at[l, pl.ds(8 * r, 8)], sems.at[i, l, r]
            )
            for i, (a, b) in enumerate(zip(ins, outs))
            for l in range(2)
            for r in range(4)
        ]
        for copy in copies:
            copy.start()
        for copy in copies:
            copy.wait()

    arrays = [pltpu.with_memory_space_constraint(a, pltpu.HBM) for a in arrays]
    return pl.pallas_call(
        body,
        in_specs=[pl.BlockSpec(memory_space=pltpu.SMEM)]
        + [pl.BlockSpec(memory_space=pl.ANY)] * (count + 1),
        out_specs=[pl.BlockSpec(memory_space=pl.ANY)] * count,
        out_shape=[pltpu.VMEM(a.shape, a.dtype) for a in arrays],
        scratch_shapes=[pltpu.SemaphoreType.DMA((count, 2, 4))],
        compiler_params=pltpu.CompilerParams(vmem_limit_bytes=4 * MIB),
        cost_estimate=pl.CostEstimate(flops=MIB, bytes_accessed=6 * MIB, transcendentals=0),
    )(where, *arrays, before)


def add(*terms):
    total = terms[0]
    for t in terms[1:]:
        total = total + t
    return total


def gate(where, value, before):
    def body(where, value, before, out):
        pass

    value = pltpu.with_memory_space_constraint(value, pltpu.VMEM)
    return pl.pallas_call(
        body,
        in_specs=[pl.BlockSpec(memory_space=pltpu.SMEM)]
        + [pl.BlockSpec(memory_space=pl.ANY)] * 2,
        out_specs=pl.BlockSpec(memory_space=pl.ANY),
        out_shape=pltpu.VMEM(value.shape, value.dtype),
        input_output_aliases={1: 0},
        compiler_params=pltpu.CompilerParams(vmem_limit_bytes=4 * MIB),
        cost_estimate=pl.CostEstimate(flops=MIB, bytes_accessed=MIB, transcendentals=0),
    )(where, value, before)


def update(where, layer, j, pieces, state, outs):
    sq, p, m, v, base = state
    clip_factor = lax.rsqrt(sq[0:1, 0:1] / (2 * 256 * 8192) + rms_eps)
    place = (where[Z] - j + 4) % 4
    for g in range(2048 // QBLOCK):
        cols = pl.ds(pl.multiple_of(j * 2048 + g * QBLOCK, QBLOCK), QBLOCK)
        clipped = clip_factor * wide(pieces[place, :, g * QBLOCK : (g + 1) * QBLOCK])
        new_m = beta_first * m[layer, :, cols] + (1.0 - beta_first) * clipped
        new_v = beta_second * v[layer, :, cols] + (1.0 - beta_second) * clipped * clipped
        old = p[layer, :, cols]
        change = -learn_rate * (new_m / (jnp.sqrt(new_v) + adam_eps) + decay_rate * old)
        outs[0][:, cols] = old + change
        outs[1][:, cols] = new_m
        outs[2][:, cols] = new_v
        delta = change + wide(base[layer, :, cols])
        scale = jnp.max(jnp.abs(delta), axis=1, keepdims=True) + scale_eps
        scale = wide(narrow(scale))
        outs[3][:, cols] = wide(narrow(delta / scale)) * scale


def update_all(where, ours, theirs, state):
    def body(where, ours, theirs, *refs):
        state, outs, held, sems = refs[:5], refs[5:9], refs[9:13], refs[13]

        def copies(side, j):
            layer = where[C] if side == 0 else 1 - where[C]
            cols = pl.ds(pl.multiple_of(j * 2048, 2048), 2048)
            return [
                pltpu.make_async_copy(
                    held[i].at[side, :, cols], outs[i].at[layer, :, cols], sems.at[i, side, j]
                )
                for i in range(4)
            ]

        for side, pieces in enumerate((ours, theirs)):

            @pl.loop(0, 4)
            def _(j, side=side, pieces=pieces):
                layer = where[C] if side == 0 else 1 - where[C]
                update(where, layer, j, pieces, state, [h.at[side] for h in held])
                for copy in copies(side, j):
                    copy.start()

        for side in range(2):
            for j in range(4):
                for copy in copies(side, j):
                    copy.wait()

    arrays = [pltpu.with_memory_space_constraint(a, pltpu.VMEM) for a in [ours, theirs, *state]]
    return pl.pallas_call(
        body,
        in_specs=[pl.BlockSpec(memory_space=pltpu.SMEM)]
        + [pl.BlockSpec(memory_space=pltpu.VMEM)] * len(arrays),
        out_specs=[pl.BlockSpec(memory_space=pl.ANY)] * 4,
        out_shape=[pltpu.HBM((2, 32, 8192), F32)] * 4,
        scratch_shapes=[pltpu.VMEM((2, 32, 8192), F32)] * 4 + [pltpu.SemaphoreType.DMA((4, 2, 4))],
        compiler_params=pltpu.CompilerParams(vmem_limit_bytes=14 * MIB),
        cost_estimate=pl.CostEstimate(flops=9 * MIB, bytes_accessed=9 * MIB, transcendentals=0),
    )(where, *arrays)


def local(partial_grads, params, moment, second_moment, snapshot):
    where = jnp.stack([lax.axis_index(name) for name in ("x", "yl", "z", "c")]).astype(jnp.int32)
    grads = partial_grads[0, 0]

    near = (1, 3, 0)
    theirs, own = fetch(grads, where, [(False, (2,)), (True, (2,))])
    got = move(theirs, c=1)
    base = narrow(params - snapshot[0])
    held_base = lax.ppermute(base, REP, [(i, (i + 1) % 16) for i in range(16)])
    theirs = fetch(grads, where, [(False, near)], (theirs, base))[0]

    def halves(where, a, b, up, down):
        up[...] = narrow(wide(a[0, 0]) + wide(b[0, 0]))
        down[...] = narrow(wide(a[0, 1]) + wide(b[0, 1]))

    up, down = vmem_call(halves, where, [own, got], [(BLOCK[1:], BF16)] * 2)
    got_near = move(gate(where, theirs, up), c=1)
    own_near = fetch(grads, where, [(True, near)], (up,))[0]
    state = preload([params, moment, second_moment], where, own_near)

    def relay(where, up, down, a, b, out_up, out_down):
        zero = jnp.zeros_like(up[...])
        over_x = where[C] == 0
        above, below = jnp.where(over_x, up[...], zero), jnp.where(over_x, zero, up[...])
        out_up[0] = narrow(wide(above) + wide(a[0, 0]) + wide(b[0, 0]))
        out_up[1] = narrow(wide(a[0, 1]) + wide(b[0, 1]))
        out_down[0] = narrow(wide(below) + wide(a[1, 0]) + wide(b[1, 0]))
        out_down[1] = narrow(wide(down[...]) + wide(a[1, 1]) + wide(b[1, 1]))

    passed = [turn(up, 0, 1, 3), turn(down, 0, 3), own_near, got_near]
    up, down = vmem_call(relay, where, passed, [(BLOCK, BF16)] * 2, (state[0],))

    def split(where, up, down, a, b, *outs):
        second = jnp.where(where[C] == 0, where[Z], where[X])
        for out, k in zip(outs, ORDER):
            j = (second + k) % 4
            total = (wide(up[:, j]) + wide(down[:, j])) + (wide(a[2, :, j]) + wide(b[2, :, j]))
            out[...] = total.astype(out.dtype)

    dims = (2, 32, 2048)
    received = [turn(up, 0, 1), turn(down, 0, 3), own_near, got_near]
    outs = [(dims, F32)] + [(dims, BF16)] * 3
    blocks = vmem_call(split, where, received, outs, (held_base,))
    blocks = [blocks[0]] + [turn(b, 1, k) for k, b in zip(ORDER[1:], blocks[1:])]

    def join(where, *refs):
        for out, index in ((refs[4], where[YL]), (refs[5], 1 - where[YL])):
            out[...] = narrow(add(*[wide(r[index]) for r in refs[:4]]))

    mine, other = vmem_call(join, where, blocks, [((32, 2048), BF16)] * 2)
    fourth = [mine, move(mine, y=2), move(other, y=1), move(other, y=3)]

    def finish(where, a, b, d, e, out):
        total = (wide(a[...]) + wide(b[...])) + (wide(d[...]) + wide(e[...]))
        squares = jnp.sum(jnp.sum(total * total, axis=0, keepdims=True), axis=1, keepdims=True)
        out[:, :2048] = narrow(total)
        high = wide(narrow(squares))
        middle = wide(narrow(squares - high))
        low = squares - high - middle
        lane = lax.broadcasted_iota(jnp.int32, (32, 128), 1)
        tail = jnp.where(lane == 0, high, jnp.where(lane == 1, middle, jnp.where(lane == 2, low, 0.0)))
        out[:, 2048:] = narrow(tail)

    piece = vmem_call(finish, where, fourth, [((32, 2176), BF16)])[0]
    ring = [piece] + [move(piece, z=k) for k in (1, 3, 2)]

    def gather(where, *refs):
        ins, out, squares = refs[:4], refs[4], refs[5]
        parts = [jnp.sum(wide(ref[:16, 2048:])[:8, :], axis=1, keepdims=True) for ref in ins]
        for k, ref in zip((0, 1, 3, 2), ins):
            out[k] = ref[:, :2048]
        total = (parts[1] + parts[2]) + (parts[0] + parts[3])
        squares[...] = jnp.broadcast_to(total, (8, 128))

    ours, squares = vmem_call(gather, where, ring, [((4, 32, 2048), BF16), ((8, 128), F32)])
    theirs = move(ours, c=1)
    side = move(squares, x=1) + move(squares, x=3)
    squares = side + (squares + move(squares, x=2))
    side = move_yl(squares) + move_yl(squares, c=1)
    squares = (squares + move(squares, c=1)) + side
    outs = update_all(where, ours, theirs, [squares, *state, held_base])
    return (outs[0], outs[1], outs[2], outs[3][None])


def solution(mesh):
    fine = Mesh(mesh.devices.reshape(2, 4, 4, 2, 2), AXES)
    row = P(None, FSDP, None)
    held = P(REP, None, FSDP, None)
    return jax.shard_map(
        local,
        mesh=fine,
        in_specs=(P(REP, FSDP, None, None, None), row, row, row, held),
        out_specs=(row, row, row, held),
        check_vma=False,
    )
```

```python
import jax
import jax.numpy as jnp
from jax import lax
from jax.experimental import pallas as pl
from jax.experimental.pallas import tpu as pltpu
from jax.sharding import Mesh, PartitionSpec as P

QBLOCK = 128
AXES = ("yl", "x", "z", "yh", "c")
FSDP = ("yl", "x")
REP = ("z", "yh", "c")
MIB = 1 << 20

beta_first = 0.9
beta_second = 0.95
learn_rate = 0.02
decay_rate = 0.1
adam_eps = 1e-08
scale_eps = 1e-06
rms_eps = 1e-06

BF16 = jnp.bfloat16
F32 = jnp.float32


def spots():
    return [
        (x, yl + 2 * yh, z, c)
        for yl in range(2)
        for x in range(4)
        for z in range(4)
        for yh in range(2)
        for c in range(2)
    ]


def rank(x, y, z, c):
    x, y, z, c = x % 4, y % 4, z % 4, c % 2
    return ((y % 2) * 4 + x) * 16 + z * 4 + (y // 2) * 2 + c


def move(value, x=0, y=0, z=0, c=0):
    pairs = [(rank(*s), rank(s[0] + x, s[1] + y, s[2] + z, s[3] + c)) for s in spots()]
    return lax.ppermute(value, AXES, pairs)


def turn(value, stage, by, by_z=None):
    by_z = by if by_z is None else by_z

    def goal(x, y, z, c):
        return rank(x + by, y, z, c) if c == stage else rank(x, y, z + by_z, c)

    return lax.ppermute(value, AXES, [(rank(*s), goal(*s)) for s in spots()])


def move_yl(value, c=0):
    pairs = [(rank(*s), rank(s[0], s[1] ^ 1, s[2], s[3] + c)) for s in spots()]
    return lax.ppermute(value, AXES, pairs)


def wide(value):
    return value.astype(F32)


def narrow(value):
    return value.astype(BF16)


def vmem_call(body, where, arrays, outs, after=()):
    count = len(arrays)

    def run(where, *refs):
        body(where, *refs[:count], *refs[count + len(after) :])

    arrays = [pltpu.with_memory_space_constraint(a, pltpu.VMEM) for a in arrays]
    return pl.pallas_call(
        run,
        in_specs=[pl.BlockSpec(memory_space=pltpu.SMEM)]
        + [pl.BlockSpec(memory_space=pltpu.VMEM)] * count
        + [pl.BlockSpec(memory_space=pl.ANY)] * len(after),
        out_specs=[pl.BlockSpec(memory_space=pltpu.VMEM)] * len(outs),
        out_shape=[pltpu.VMEM(dims, kind) for dims, kind in outs],
        compiler_params=pltpu.CompilerParams(vmem_limit_bytes=12 * MIB),
        cost_estimate=pl.CostEstimate(flops=4 * MIB, bytes_accessed=4 * MIB, transcendentals=0),
    )(where, *arrays, *after)


BLOCK = (2, 4, 32, 2048)
ORDER = (0, 2, 1, 3)

X, YL, Z, C = range(4)


def fetch(grads, where, wanted, after=()):
    def body(where, src, *refs):
        outs, sems = refs[len(after) : -1], refs[-1]
        copies = []
        for out, (own, offsets) in zip(outs, wanted):
            layer = where[C] if own else 1 - where[C]
            over_x = layer == 0
            for i, k in enumerate(offsets):
                for yl in range(2):
                    for j in range(4):
                        row = jnp.where(over_x, (where[X] + k) % 4, j)
                        col = jnp.where(over_x, j, (where[Z] + k) % 4)
                        cols = pl.ds(pl.multiple_of(col * 2048, 2048), 2048)
                        copies.append((src.at[layer, yl, row, :, cols], out.at[i, yl, j]))
        copies = [pltpu.make_async_copy(a, b, sems.at[i]) for i, (a, b) in enumerate(copies)]
        for copy in copies:
            copy.start()
        for copy in copies:
            copy.wait()

    blocks = sum(len(offsets) for _, offsets in wanted)
    grads = pltpu.with_memory_space_constraint(grads.reshape(2, 2, 4, 32, 8192), pltpu.HBM)
    return pl.pallas_call(
        body,
        in_specs=[pl.BlockSpec(memory_space=pltpu.SMEM)]
        + [pl.BlockSpec(memory_space=pl.ANY)] * (1 + len(after)),
        out_specs=[pl.BlockSpec(memory_space=pl.ANY)] * len(wanted),
        out_shape=[pltpu.VMEM((len(offsets),) + BLOCK, BF16) for _, offsets in wanted],
        scratch_shapes=[pltpu.SemaphoreType.DMA((8 * blocks,))],
        compiler_params=pltpu.CompilerParams(vmem_limit_bytes=4 * MIB),
        cost_estimate=pl.CostEstimate(flops=0, bytes_accessed=blocks * MIB, transcendentals=0),
    )(where, grads, *after)


def preload(arrays, where, *before):
    count = len(arrays)

    def body(where, *refs):
        ins, outs, sems = refs[:count], refs[-1 - count : -1], refs[-1]
        copies = [
            pltpu.make_async_copy(
                a.at[l, pl.ds(8 * r, 8)], b.at[l, pl.ds(8 * r, 8)], sems.at[i, l, r]
            )
            for i, (a, b) in enumerate(zip(ins, outs))
            for l in range(2)
            for r in range(4)
        ]
        for copy in copies:
            copy.start()
        for copy in copies:
            copy.wait()

    arrays = [pltpu.with_memory_space_constraint(a, pltpu.HBM) for a in arrays]
    return pl.pallas_call(
        body,
        in_specs=[pl.BlockSpec(memory_space=pltpu.SMEM)]
        + [pl.BlockSpec(memory_space=pl.ANY)] * (count + len(before)),
        out_specs=[pl.BlockSpec(memory_space=pl.ANY)] * count,
        out_shape=[pltpu.VMEM(a.shape, a.dtype) for a in arrays],
        scratch_shapes=[pltpu.SemaphoreType.DMA((count, 2, 4))],
        compiler_params=pltpu.CompilerParams(vmem_limit_bytes=4 * MIB),
        cost_estimate=pl.CostEstimate(flops=MIB, bytes_accessed=6 * MIB, transcendentals=0),
    )(where, *arrays, *before)


def add(*terms):
    total = terms[0]
    for t in terms[1:]:
        total = total + t
    return total


def update(where, layer, j, pieces, state, outs):
    sq, p, m, v, base = state
    clip_factor = lax.rsqrt(sq[0:1, 0:1] / (2 * 256 * 8192) + rms_eps)
    place = (where[Z] - j + 4) % 4
    first_gain = (1.0 - beta_first) * clip_factor
    second_gain = (1.0 - beta_second) * clip_factor * clip_factor
    for g in range(2048 // QBLOCK):
        cols = pl.ds(pl.multiple_of(j * 2048 + g * QBLOCK, QBLOCK), QBLOCK)
        summed = wide(pieces[place, :, g * QBLOCK : (g + 1) * QBLOCK])
        new_m = beta_first * m[layer, :, cols] + first_gain * summed
        new_v = beta_second * v[layer, :, cols] + second_gain * summed * summed
        root = new_v * lax.rsqrt(new_v)
        old = p[layer, :, cols]
        change = -learn_rate * (new_m / (root + adam_eps) + decay_rate * old)
        outs[0][:, cols] = old + change
        outs[1][:, cols] = new_m
        outs[2][:, cols] = new_v
        delta = change + wide(base[layer, :, cols])
        scale = jnp.max(jnp.abs(delta), axis=1, keepdims=True) + scale_eps
        scale = wide(narrow(scale))
        held = wide(narrow(delta * (1.0 / scale)))
        outs[3][:, cols] = held * scale


def update_all(where, ours, theirs, state):
    def body(where, ours, theirs, *refs):
        state, outs, held, sems = refs[:5], refs[5:9], refs[9:13], refs[13]

        def copies(side, j):
            layer = where[C] if side == 0 else 1 - where[C]
            cols = pl.ds(pl.multiple_of(j * 2048, 2048), 2048)
            return [
                pltpu.make_async_copy(
                    held[i].at[side, :, cols], outs[i].at[layer, :, cols], sems.at[i, side, j]
                )
                for i in range(4)
            ]

        for side, pieces in enumerate((ours, theirs)):

            @pl.loop(0, 4)
            def _(j, side=side, pieces=pieces):
                layer = where[C] if side == 0 else 1 - where[C]
                update(where, layer, j, pieces, state, [h.at[side] for h in held])
                for copy in copies(side, j):
                    copy.start()

        for side in range(2):
            for j in range(4):
                for copy in copies(side, j):
                    copy.wait()

    arrays = [pltpu.with_memory_space_constraint(a, pltpu.VMEM) for a in [ours, theirs, *state]]
    return pl.pallas_call(
        body,
        in_specs=[pl.BlockSpec(memory_space=pltpu.SMEM)]
        + [pl.BlockSpec(memory_space=pltpu.VMEM)] * len(arrays),
        out_specs=[pl.BlockSpec(memory_space=pl.ANY)] * 4,
        out_shape=[pltpu.HBM((2, 32, 8192), F32)] * 4,
        scratch_shapes=[pltpu.VMEM((2, 32, 8192), F32)] * 4 + [pltpu.SemaphoreType.DMA((4, 2, 4))],
        compiler_params=pltpu.CompilerParams(vmem_limit_bytes=14 * MIB),
        cost_estimate=pl.CostEstimate(flops=9 * MIB, bytes_accessed=9 * MIB, transcendentals=0),
    )(where, *arrays)


def local(partial_grads, params, moment, second_moment, snapshot):
    where = jnp.stack([lax.axis_index(name) for name in ("x", "yl", "z", "c")]).astype(jnp.int32)
    grads = partial_grads[0, 0]

    near = (1, 3, 0)
    theirs, own = fetch(grads, where, [(False, (2,)), (True, (2,))])
    got = move(theirs, c=1)
    base = narrow(params - snapshot[0])
    held_base = lax.ppermute(base, REP, [(i, (i + 1) % 16) for i in range(16)])
    theirs = fetch(grads, where, [(False, near)], (theirs, base))[0]

    def halves(where, a, b, rest, up, down, same):
        up[...] = narrow(wide(a[0, 0]) + wide(b[0, 0]))
        down[...] = narrow(wide(a[0, 1]) + wide(b[0, 1]))

    passed = [pltpu.with_memory_space_constraint(r, pltpu.VMEM) for r in (own, got, theirs)]
    up, down, theirs = pl.pallas_call(
        halves,
        in_specs=[pl.BlockSpec(memory_space=pltpu.SMEM)]
        + [pl.BlockSpec(memory_space=pltpu.VMEM)] * 2
        + [pl.BlockSpec(memory_space=pl.ANY)],
        out_specs=[pl.BlockSpec(memory_space=pltpu.VMEM)] * 2 + [pl.BlockSpec(memory_space=pl.ANY)],
        out_shape=[pltpu.VMEM(BLOCK[1:], BF16)] * 2 + [pltpu.VMEM(theirs.shape, BF16)],
        input_output_aliases={3: 2},
        compiler_params=pltpu.CompilerParams(vmem_limit_bytes=12 * MIB),
        cost_estimate=pl.CostEstimate(flops=4 * MIB, bytes_accessed=4 * MIB, transcendentals=0),
    )(where, *passed)
    got_near = move(theirs, c=1)
    own_near = fetch(grads, where, [(True, near)], (up,))[0]

    def relay_down(where, down, a, b, out, up_1):
        out[...] = narrow(wide(down[...]) + wide(a[1, 1]) + wide(b[1, 1]))
        up_1[...] = narrow(wide(a[0, 1]) + wide(b[0, 1]))

    passed = [turn(down, 0, 3), own_near, got_near]
    down, up_1 = vmem_call(relay_down, where, passed, [(BLOCK[1:], BF16)] * 2)

    def relay_up(where, up, a, b, other, up_0):
        zero = jnp.zeros_like(up[...])
        over_x = where[C] == 0
        above, below = jnp.where(over_x, up[...], zero), jnp.where(over_x, zero, up[...])
        other[...] = narrow(wide(below) + wide(a[1, 0]) + wide(b[1, 0]))
        up_0[...] = narrow(wide(above) + wide(a[0, 0]) + wide(b[0, 0]))

    passed = [turn(up, 0, 1, 3), own_near, got_near]
    outs = [(BLOCK[1:], BF16)] * 2
    other, up_0 = vmem_call(relay_up, where, passed, outs, (down,))

    def split(where, first, second, up_0, up_1, a, b, *outs):
        axis = jnp.where(where[C] == 0, where[Z], where[X])
        for out, k in zip(outs, ORDER):
            j = (axis + k) % 4
            for yl, (up, down) in enumerate(((up_0, second), (up_1, first))):
                total = (wide(up[j]) + wide(down[j])) + (wide(a[2, yl, j]) + wide(b[2, yl, j]))
                out[yl] = total.astype(out.dtype)

    dims = (2, 32, 2048)
    received = [turn(down, 0, 3), turn(other, 0, 3), turn(up_0, 0, 1), turn(up_1, 0, 1)]
    state = preload([params, moment, second_moment], where, received[0], received[3])
    outs = [(dims, F32)] + [(dims, BF16)] * 3
    received += [own_near, got_near]
    blocks = vmem_call(split, where, received, outs, (held_base, state[0]))
    blocks = [blocks[0]] + [turn(b, 1, k) for k, b in zip(ORDER[1:], blocks[1:])]

    def join(where, *refs):
        for out, index in ((refs[4], where[YL]), (refs[5], 1 - where[YL])):
            out[...] = narrow(add(*[wide(r[index]) for r in refs[:4]]))

    mine, other = vmem_call(join, where, blocks, [((32, 2048), BF16)] * 2)
    fourth = [mine, move(mine, y=2), move(other, y=1), move(other, y=3)]

    def finish(where, a, b, d, e, out):
        total = (wide(a[...]) + wide(b[...])) + (wide(d[...]) + wide(e[...]))
        squares = jnp.sum(jnp.sum(total * total, axis=0, keepdims=True), axis=1, keepdims=True)
        out[:, :2048] = narrow(total)
        high = wide(narrow(squares))
        middle = wide(narrow(squares - high))
        low = squares - high - middle
        lane = lax.broadcasted_iota(jnp.int32, (32, 128), 1)
        tail = jnp.where(lane == 0, high, jnp.where(lane == 1, middle, jnp.where(lane == 2, low, 0.0)))
        out[:, 2048:] = narrow(tail)

    piece = vmem_call(finish, where, fourth, [((32, 2176), BF16)])[0]
    ring = [piece] + [move(piece, z=k) for k in (1, 3, 2)]

    def gather(where, *refs):
        ins, out, squares = refs[:4], refs[4], refs[5]
        parts = [jnp.sum(wide(ref[:16, 2048:])[:8, :], axis=1, keepdims=True) for ref in ins]
        for k, ref in zip((0, 1, 3, 2), ins):
            out[k] = ref[:, :2048]
        total = (parts[1] + parts[2]) + (parts[0] + parts[3])
        squares[...] = jnp.broadcast_to(total, (8, 128))

    ours, squares = vmem_call(gather, where, ring, [((4, 32, 2048), BF16), ((8, 128), F32)])
    theirs = move(ours, c=1)
    side = move(squares, x=1) + move(squares, x=3)
    squares = side + (squares + move(squares, x=2))
    side = move_yl(squares) + move_yl(squares, c=1)
    squares = (squares + move(squares, c=1)) + side
    outs = update_all(where, ours, theirs, [squares, *state, held_base])
    return (outs[0], outs[1], outs[2], outs[3][None])


def solution(mesh):
    fine = Mesh(mesh.devices.reshape(2, 4, 4, 2, 2), AXES)
    row = P(None, FSDP, None)
    held = P(REP, None, FSDP, None)
    return jax.shard_map(
        local,
        mesh=fine,
        in_specs=(P(REP, FSDP, None, None, None), row, row, row, held),
        out_specs=(row, row, row, held),
        check_vma=False,
    )
```

```python
import jax
import jax.numpy as jnp
from jax import lax
from jax.experimental import pallas as pl
from jax.experimental.pallas import tpu as pltpu
from jax.sharding import Mesh, PartitionSpec as P

QBLOCK = 128
AXES = ("yl", "x", "z", "yh", "c")
FSDP = ("yl", "x")
REP = ("z", "yh", "c")
MIB = 1 << 20

beta_first = 0.9
beta_second = 0.95
learn_rate = 0.02
decay_rate = 0.1
adam_eps = 1e-08
scale_eps = 1e-06
rms_eps = 1e-06

BF16 = jnp.bfloat16
F32 = jnp.float32


def spots():
    return [
        (x, yl + 2 * yh, z, c)
        for yl in range(2)
        for x in range(4)
        for z in range(4)
        for yh in range(2)
        for c in range(2)
    ]


def rank(x, y, z, c):
    x, y, z, c = x % 4, y % 4, z % 4, c % 2
    return ((y % 2) * 4 + x) * 16 + z * 4 + (y // 2) * 2 + c


def move(value, x=0, y=0, z=0, c=0):
    pairs = [(rank(*s), rank(s[0] + x, s[1] + y, s[2] + z, s[3] + c)) for s in spots()]
    return lax.ppermute(value, AXES, pairs)


def turn(value, stage, by, by_z=None):
    by_z = by if by_z is None else by_z

    def goal(x, y, z, c):
        return rank(x + by, y, z, c) if c == stage else rank(x, y, z + by_z, c)

    return lax.ppermute(value, AXES, [(rank(*s), goal(*s)) for s in spots()])


def move_yl(value, c=0):
    pairs = [(rank(*s), rank(s[0], s[1] ^ 1, s[2], s[3] + c)) for s in spots()]
    return lax.ppermute(value, AXES, pairs)


def wide(value):
    return value.astype(F32)


def narrow(value):
    return value.astype(BF16)


def vmem_call(body, where, arrays, outs, after=()):
    count = len(arrays)

    def run(where, *refs):
        body(where, *refs[:count], *refs[count + len(after) :])

    arrays = [pltpu.with_memory_space_constraint(a, pltpu.VMEM) for a in arrays]
    return pl.pallas_call(
        run,
        in_specs=[pl.BlockSpec(memory_space=pltpu.SMEM)]
        + [pl.BlockSpec(memory_space=pltpu.VMEM)] * count
        + [pl.BlockSpec(memory_space=pl.ANY)] * len(after),
        out_specs=[pl.BlockSpec(memory_space=pltpu.VMEM)] * len(outs),
        out_shape=[pltpu.VMEM(dims, kind) for dims, kind in outs],
        compiler_params=pltpu.CompilerParams(vmem_limit_bytes=12 * MIB),
        cost_estimate=pl.CostEstimate(flops=4 * MIB, bytes_accessed=4 * MIB, transcendentals=0),
    )(where, *arrays, *after)


BLOCK = (2, 4, 32, 2048)
ORDER = (0, 2, 1, 3)

X, YL, Z, C = range(4)


def fetch(grads, where, wanted, after=()):
    def body(where, src, *refs):
        outs, sems = refs[len(after) : -1], refs[-1]
        copies = []
        for out, (own, offsets) in zip(outs, wanted):
            layer = where[C] if own else 1 - where[C]
            over_x = layer == 0
            for i, k in enumerate(offsets):
                for yl in range(2):
                    for j in range(4):
                        row = jnp.where(over_x, (where[X] + k) % 4, j)
                        col = jnp.where(over_x, j, (where[Z] + k) % 4)
                        cols = pl.ds(pl.multiple_of(col * 2048, 2048), 2048)
                        copies.append((src.at[layer, yl, row, :, cols], out.at[i, yl, j]))
        copies = [pltpu.make_async_copy(a, b, sems.at[i]) for i, (a, b) in enumerate(copies)]
        for copy in copies:
            copy.start()
        for copy in copies:
            copy.wait()

    blocks = sum(len(offsets) for _, offsets in wanted)
    grads = pltpu.with_memory_space_constraint(grads.reshape(2, 2, 4, 32, 8192), pltpu.HBM)
    return pl.pallas_call(
        body,
        in_specs=[pl.BlockSpec(memory_space=pltpu.SMEM)]
        + [pl.BlockSpec(memory_space=pl.ANY)] * (1 + len(after)),
        out_specs=[pl.BlockSpec(memory_space=pl.ANY)] * len(wanted),
        out_shape=[pltpu.VMEM((len(offsets),) + BLOCK, BF16) for _, offsets in wanted],
        scratch_shapes=[pltpu.SemaphoreType.DMA((8 * blocks,))],
        compiler_params=pltpu.CompilerParams(vmem_limit_bytes=4 * MIB),
        cost_estimate=pl.CostEstimate(flops=0, bytes_accessed=blocks * MIB, transcendentals=0),
    )(where, grads, *after)


def preload(arrays, where, *before):
    count = len(arrays)

    def body(where, *refs):
        ins, outs, sems = refs[:count], refs[-1 - count : -1], refs[-1]
        copies = [
            pltpu.make_async_copy(
                a.at[l, pl.ds(8 * r, 8)], b.at[l, pl.ds(8 * r, 8)], sems.at[i, l, r]
            )
            for i, (a, b) in enumerate(zip(ins, outs))
            for l in range(2)
            for r in range(4)
        ]
        for copy in copies:
            copy.start()
        for copy in copies:
            copy.wait()

    arrays = [pltpu.with_memory_space_constraint(a, pltpu.HBM) for a in arrays]
    return pl.pallas_call(
        body,
        in_specs=[pl.BlockSpec(memory_space=pltpu.SMEM)]
        + [pl.BlockSpec(memory_space=pl.ANY)] * (count + len(before)),
        out_specs=[pl.BlockSpec(memory_space=pl.ANY)] * count,
        out_shape=[pltpu.VMEM(a.shape, a.dtype) for a in arrays],
        scratch_shapes=[pltpu.SemaphoreType.DMA((count, 2, 4))],
        compiler_params=pltpu.CompilerParams(vmem_limit_bytes=4 * MIB),
        cost_estimate=pl.CostEstimate(flops=MIB, bytes_accessed=6 * MIB, transcendentals=0),
    )(where, *arrays, *before)


def add(*terms):
    total = terms[0]
    for t in terms[1:]:
        total = total + t
    return total


def update(where, layer, j, pieces, state, outs):
    sq, p, m, v, base = state
    clip_factor = lax.rsqrt(sq[0:1, 0:1] / (2 * 256 * 8192) + rms_eps)
    place = (where[Z] - j + 4) % 4
    first_gain = (1.0 - beta_first) * clip_factor
    second_gain = (1.0 - beta_second) * clip_factor * clip_factor
    for g in range(2048 // QBLOCK):
        cols = pl.ds(pl.multiple_of(j * 2048 + g * QBLOCK, QBLOCK), QBLOCK)
        summed = wide(pieces[place, :, g * QBLOCK : (g + 1) * QBLOCK])
        new_m = beta_first * m[layer, :, cols] + first_gain * summed
        new_v = beta_second * v[layer, :, cols] + second_gain * summed * summed
        root = new_v * lax.rsqrt(new_v)
        old = p[layer, :, cols]
        change = -learn_rate * (new_m / (root + adam_eps) + decay_rate * old)
        outs[0][:, cols] = old + change
        outs[1][:, cols] = new_m
        outs[2][:, cols] = new_v
        delta = change + wide(base[layer, :, cols])
        scale = jnp.max(jnp.abs(delta), axis=1, keepdims=True) + scale_eps
        scale = wide(narrow(scale))
        held = wide(narrow(delta * (1.0 / scale)))
        outs[3][:, cols] = held * scale


def update_all(where, ours, theirs, state):
    def body(where, ours, theirs, *refs):
        state, outs, held, sems = refs[:5], refs[5:9], refs[9:13], refs[13]

        def copies(side, j):
            layer = where[C] if side == 0 else 1 - where[C]
            cols = pl.ds(pl.multiple_of(j * 2048, 2048), 2048)
            return [
                pltpu.make_async_copy(
                    held[i].at[side, :, cols], outs[i].at[layer, :, cols], sems.at[i, side, j]
                )
                for i in range(4)
            ]

        for side, pieces in enumerate((ours, theirs)):

            @pl.loop(0, 4, unroll=True)
            def _(j, side=side, pieces=pieces):
                layer = where[C] if side == 0 else 1 - where[C]
                update(where, layer, j, pieces, state, [h.at[side] for h in held])
                for copy in copies(side, j):
                    copy.start()

        for side in range(2):
            for j in range(4):
                for copy in copies(side, j):
                    copy.wait()

    arrays = [pltpu.with_memory_space_constraint(a, pltpu.VMEM) for a in [ours, theirs, *state]]
    return pl.pallas_call(
        body,
        in_specs=[pl.BlockSpec(memory_space=pltpu.SMEM)]
        + [pl.BlockSpec(memory_space=pltpu.VMEM)] * len(arrays),
        out_specs=[pl.BlockSpec(memory_space=pl.ANY)] * 4,
        out_shape=[pltpu.HBM((2, 32, 8192), F32)] * 4,
        scratch_shapes=[pltpu.VMEM((2, 32, 8192), F32)] * 4 + [pltpu.SemaphoreType.DMA((4, 2, 4))],
        compiler_params=pltpu.CompilerParams(vmem_limit_bytes=14 * MIB),
        cost_estimate=pl.CostEstimate(flops=9 * MIB, bytes_accessed=9 * MIB, transcendentals=0),
    )(where, *arrays)


def local(partial_grads, params, moment, second_moment, snapshot):
    where = jnp.stack([lax.axis_index(name) for name in ("x", "yl", "z", "c")]).astype(jnp.int32)
    grads = partial_grads[0, 0]

    near = (1, 3, 0)
    theirs, own = fetch(grads, where, [(False, (2,)), (True, (2,))])
    got = move(theirs, c=1)
    base = narrow(params - snapshot[0])
    held_base = lax.ppermute(base, REP, [(i, (i + 1) % 16) for i in range(16)])
    theirs = fetch(grads, where, [(False, near)], (theirs, base))[0]

    def halves(where, a, b, rest, up, down, same):
        up[...] = narrow(wide(a[0, 0]) + wide(b[0, 0]))
        down[...] = narrow(wide(a[0, 1]) + wide(b[0, 1]))

    passed = [pltpu.with_memory_space_constraint(r, pltpu.VMEM) for r in (own, got, theirs)]
    up, down, theirs = pl.pallas_call(
        halves,
        in_specs=[pl.BlockSpec(memory_space=pltpu.SMEM)]
        + [pl.BlockSpec(memory_space=pltpu.VMEM)] * 2
        + [pl.BlockSpec(memory_space=pl.ANY)],
        out_specs=[pl.BlockSpec(memory_space=pltpu.VMEM)] * 2 + [pl.BlockSpec(memory_space=pl.ANY)],
        out_shape=[pltpu.VMEM(BLOCK[1:], BF16)] * 2 + [pltpu.VMEM(theirs.shape, BF16)],
        input_output_aliases={3: 2},
        compiler_params=pltpu.CompilerParams(vmem_limit_bytes=12 * MIB),
        cost_estimate=pl.CostEstimate(flops=4 * MIB, bytes_accessed=4 * MIB, transcendentals=0),
    )(where, *passed)
    got_near = move(theirs, c=1)
    own_near = fetch(grads, where, [(True, near)], (up,))[0]

    def relay_down(where, down, a, b, out, up_1):
        out[...] = narrow(wide(down[...]) + wide(a[1, 1]) + wide(b[1, 1]))
        up_1[...] = narrow(wide(a[0, 1]) + wide(b[0, 1]))

    passed = [turn(down, 0, 3), own_near, got_near]
    down, up_1 = vmem_call(relay_down, where, passed, [(BLOCK[1:], BF16)] * 2)

    def relay_up(where, up, a, b, other, up_0):
        zero = jnp.zeros_like(up[...])
        over_x = where[C] == 0
        above, below = jnp.where(over_x, up[...], zero), jnp.where(over_x, zero, up[...])
        other[...] = narrow(wide(below) + wide(a[1, 0]) + wide(b[1, 0]))
        up_0[...] = narrow(wide(above) + wide(a[0, 0]) + wide(b[0, 0]))

    passed = [turn(up, 0, 1, 3), own_near, got_near]
    outs = [(BLOCK[1:], BF16)] * 2
    other, up_0 = vmem_call(relay_up, where, passed, outs, (down,))

    def split(where, first, second, up_0, up_1, a, b, *outs):
        axis = jnp.where(where[C] == 0, where[Z], where[X])
        for out, k in zip(outs, ORDER):
            j = (axis + k) % 4
            for yl, (up, down) in enumerate(((up_0, second), (up_1, first))):
                total = (wide(up[j]) + wide(down[j])) + (wide(a[2, yl, j]) + wide(b[2, yl, j]))
                out[yl] = total.astype(out.dtype)

    dims = (2, 32, 2048)
    received = [turn(down, 0, 3), turn(other, 0, 3), turn(up_0, 0, 1), turn(up_1, 0, 1)]
    state = preload([params, moment, second_moment], where, received[0], received[3])
    outs = [(dims, F32)] + [(dims, BF16)] * 3
    received += [own_near, got_near]
    blocks = vmem_call(split, where, received, outs, (held_base, state[0]))
    blocks = [blocks[0]] + [turn(b, 1, k) for k, b in zip(ORDER[1:], blocks[1:])]

    def join(where, *refs):
        for out, index in ((refs[4], where[YL]), (refs[5], 1 - where[YL])):
            out[...] = narrow(add(*[wide(r[index]) for r in refs[:4]]))

    mine, other = vmem_call(join, where, blocks, [((32, 2048), BF16)] * 2)
    fourth = [mine, move(mine, y=2), move(other, y=1), move(other, y=3)]

    def finish(where, a, b, d, e, out):
        total = (wide(a[...]) + wide(b[...])) + (wide(d[...]) + wide(e[...]))
        squares = jnp.sum(jnp.sum(total * total, axis=0, keepdims=True), axis=1, keepdims=True)
        out[:, :2048] = narrow(total)
        high = wide(narrow(squares))
        middle = wide(narrow(squares - high))
        low = squares - high - middle
        lane = lax.broadcasted_iota(jnp.int32, (32, 128), 1)
        tail = jnp.where(lane == 0, high, jnp.where(lane == 1, middle, jnp.where(lane == 2, low, 0.0)))
        out[:, 2048:] = narrow(tail)

    piece = vmem_call(finish, where, fourth, [((32, 2176), BF16)])[0]
    ring = [piece] + [move(piece, z=k) for k in (1, 3, 2)]

    def gather(where, *refs):
        ins, out, squares = refs[:4], refs[4], refs[5]
        parts = [jnp.sum(wide(ref[:16, 2048:])[:8, :], axis=1, keepdims=True) for ref in ins]
        for k, ref in zip((0, 1, 3, 2), ins):
            out[k] = ref[:, :2048]
        total = (parts[1] + parts[2]) + (parts[0] + parts[3])
        squares[...] = jnp.broadcast_to(total, (8, 128))

    ours, squares = vmem_call(gather, where, ring, [((4, 32, 2048), BF16), ((8, 128), F32)])
    theirs = move(ours, c=1)
    side = move(squares, x=1) + move(squares, x=3)
    squares = side + (squares + move(squares, x=2))
    side = move_yl(squares) + move_yl(squares, c=1)
    squares = (squares + move(squares, c=1)) + side
    outs = update_all(where, ours, theirs, [squares, *state, held_base])
    return (outs[0], outs[1], outs[2], outs[3][None])


def solution(mesh):
    fine = Mesh(mesh.devices.reshape(2, 4, 4, 2, 2), AXES)
    row = P(None, FSDP, None)
    held = P(REP, None, FSDP, None)
    return jax.shard_map(
        local,
        mesh=fine,
        in_specs=(P(REP, FSDP, None, None, None), row, row, row, held),
        out_specs=(row, row, row, held),
        check_vma=False,
    )
```
